32 devices in a mesh: groups: 2 (over y), slab: 16 (over z, x, core).
Axes of the slice: x: 2, y: 2, z: 4, core: 2. Of those that a mesh axis runs over, the one named last changes fastest.
Arguments:
- mobile: float32 [24, 393216], P(None, ('groups', 'slab')), parts along dimension 1, may hold values from 0 to 2
- immobile: bfloat16 [8, 24, 393216], P(None, None, ('groups', 'slab')), parts along dimension 2, may hold values from 0 to 2
- courant: float32 [393216], P(('groups', 'slab')), parts along dimension 0, may hold values from 0.4 to 0.85
- exchange_rate: float32 [8], replicated, may hold values from 0.01 to 0.25
- capacity: float32 [8], replicated, may hold values from 0.05 to 0.3
- reaction: float32 [24, 24], replicated, may hold values from -1 to 1
- precip_rate: float32 [24], replicated, may hold values from 0.3 to 3
- block_class: int32 [3072], P(('groups', 'slab')), parts along dimension 0, may hold values from 0 to 1, as said below
- precip_mask: int32 [393216], P(('groups', 'slab')), parts along dimension 0, may hold values 0 or 1
Outputs:
- mobile_out: float32 [24, 393216], P(None, ('groups', 'slab')), parts along dimension 1
- immobile_out: bfloat16 [8, 24, 393216], P(None, None, ('groups', 'slab')), parts along dimension 2
The draws below stay inside these ranges and needn't reach their ends.
There are 2 independent parts, one for each index of `groups`. The reference program is written for one: setup_inputs(seed, part) draws one part's arguments, and reference() takes and returns one part's arrays. A program takes and returns all parts, laid end to end along the dimension named above; an argument that names none is the same for every part. Nothing has to cross between parts.
Inputs may be any that keep to these rules, and one draw needn't show every extreme that they name: `block_class`: 1 marks a block in a precipitation zone; zones are runs of neighbouring blocks.
All inputs are finite; a program needn't handle non-finite values. No bound on the sum of `precip_mask` on one device may be relied on, other than what follows from the above.
Results may differ from the reference program's by a relative error of at most 0.001.
Values sent between devices are 32-bit elements; how exact they have to be, the bound alone decides.
A program may use at most 64 MiB of HBM per device.

```python
import math
import jax
import jax.numpy as jnp
from jax import lax

SPECIES = 24
CLASSES = 8
BLOCK = 128
TSTEPS = 4
NEWTON = 3
SUBSTEPS = 20
CELLS = 196608
NBLOCKS = 1536


def draw_block_class(key, part):
    key = jax.random.fold_in(key, 11)
    centers = jax.random.randint(key, (4,), 0, NBLOCKS)
    span = max(1, NBLOCKS // 40)
    index = jnp.arange(NBLOCKS, dtype=jnp.int32)
    offset = (index[None, :] - centers[:, None]) % NBLOCKS
    inside = offset < 2 * span
    return jnp.any(inside, axis=0).astype(jnp.int32)


def draw_reaction(key, part):
    key = jax.random.fold_in(key, 23)
    sigma = 0.8 / math.sqrt(SPECIES)
    values = jnp.clip(jax.random.normal(key, (SPECIES, SPECIES), jnp.float32), -5.0, 5.0)
    return values * sigma


def set_ends(result, key, least, largest):
    place = [jax.random.randint(jax.random.fold_in(key, axis), (), 0, length) for axis, length in enumerate(result.shape)]
    longest = result.shape.index(max(result.shape))
    neighbour = place[:longest] + [(place[longest] + 1) % result.shape[longest]] + place[longest + 1:]
    return result.at[tuple(place)].set(least).at[tuple(neighbour)].set(largest)


def block_scale(own_key, extent, shards, smallest, high):
    level, own = 1.0, jax.random.fold_in(own_key, 6)
    for dim, parts in shards:
        heights = jnp.exp(jax.random.uniform(jax.random.fold_in(own, dim), (parts,), jnp.float32, smallest / len(shards), high / len(shards)))
        level = level * jnp.repeat(heights, extent[dim] // parts).reshape([-1 if axis == dim else 1 for axis in range(len(extent))])
    return level


def setup_inputs(seed: int = 0, part: int = 0) -> dict:
    arg_keys = jax.random.split(jax.random.key(seed), 10)
    part_splits = jax.random.split(jax.random.fold_in(arg_keys[9], part), 10)
    return {
        "mobile": jnp.clip(2.0 * jax.random.uniform(part_splits[0], (SPECIES, CELLS), jnp.float32) ** block_scale(part_splits[0], (SPECIES, CELLS), ((1, 16),), -0.2, 0.2), 0.0, 2.0),
        "immobile": jnp.clip(2.0 * jax.random.uniform(part_splits[1], (CLASSES, SPECIES, CELLS), jnp.float32) ** block_scale(part_splits[1], (CLASSES, SPECIES, CELLS), ((2, 16),), -0.2, 0.2), 0.0, 2.0).astype(jnp.bfloat16),
        "courant": jnp.clip(0.4 + 0.45000002 * jax.random.uniform(part_splits[2], (CELLS,), jnp.float32) ** block_scale(part_splits[2], (CELLS,), ((0, 16),), -0.2, 0.2), 0.4, 0.85),
        "exchange_rate": jnp.clip(jnp.exp(jax.random.uniform(arg_keys[3], (CLASSES,), jnp.float32, math.log(0.01), math.log(0.25))), 0.01, 0.25),
        "capacity": jnp.clip(jax.random.uniform(arg_keys[4], (CLASSES,), jnp.float32, 0.05, 0.3), 0.05, 0.3),
        "reaction": draw_reaction(jax.random.fold_in(arg_keys[9], 71), part),
        "precip_rate": jnp.clip(jnp.exp(jax.random.uniform(arg_keys[6], (SPECIES,), jnp.float32, math.log(0.3), math.log(3.0))), 0.3, 3.0),
        "block_class": draw_block_class(jax.random.fold_in(jax.random.fold_in(arg_keys[9], part), 71), part),
        "precip_mask": set_ends((jax.random.randint(part_splits[8], (CELLS,), 0, 2) < 1).astype(jnp.int32), jax.random.fold_in(part_splits[8], 1), 0, 1),
    }


dispersion = 0.05
reaction_step = 0.25
heavy_span = 4.0


def newton(conc, mask_f, step_h, reaction, rates):
    guess = conc
    for turn in range(NEWTON):
        driven = jnp.einsum('st,tbc->sbc', reaction, guess, precision=lax.Precision.HIGHEST) - guess
        resid = guess - conc - step_h * (driven - mask_f * rates * jax.nn.softplus(guess))
        scaled = 1.0 / (1.0 + step_h * mask_f * rates * jax.nn.sigmoid(guess))
        first = scaled * resid
        coupled = jnp.einsum('st,tbc->sbc', reaction, first, precision=lax.Precision.HIGHEST) - first
        guess = guess - (first + scaled * step_h * coupled)
    return guess


def reference(mobile, immobile, courant, exchange_rate, capacity, reaction, precip_rate, block_class, precip_mask):
    moving = mobile
    fixed_zone = immobile.astype(jnp.float32)
    rates = exchange_rate[:, None, None]
    ratios = capacity[:, None, None]
    for step in range(TSTEPS):
        padded = jnp.pad(moving, ((0, 0), (1, 1)))
        center = padded[:, 1:-1]
        left = padded[:, :-2]
        right = padded[:, 2:]
        transfer = jnp.sum(ratios * rates * (fixed_zone - center[None]), axis=0)
        new_moving = center - courant[None, :] * (center - left) + dispersion * (right - 2.0 * center + left) + transfer
        fixed_zone = fixed_zone + rates * (center[None] - fixed_zone)
        moving = new_moving
    conc = moving.reshape(SPECIES, NBLOCKS, BLOCK)
    mask_f = precip_mask.reshape(1, NBLOCKS, BLOCK).astype(jnp.float32)
    heavy = block_class.reshape(1, NBLOCKS, 1) == 1
    step_h = jnp.where(heavy, heavy_span / SUBSTEPS, reaction_step)
    substeps = jnp.where(heavy, SUBSTEPS, 1)
    species_rates = precip_rate[:, None, None]

    def one_sub(index, guess):
        return newton(guess, mask_f, jnp.where(index < substeps, step_h, 0.0), reaction, species_rates)

    reacted = lax.fori_loop(0, SUBSTEPS, one_sub, conc)
    return reacted.reshape(SPECIES, CELLS), fixed_zone.astype(jnp.bfloat16)
```

```python
from functools import partial

import jax
import jax.numpy as jnp
from jax import lax
from jax.experimental import pallas as pl
from jax.experimental.pallas import tpu as pltpu
from jax.sharding import PartitionSpec as P

BLOCK = 128
TSTEPS = 4
NEWTON = 3
SUBSTEPS = 20

dispersion = 0.05
reaction_step = 0.25
heavy_span = 4.0

EDGE = 128
CLASSES = 8
SPECIES = 24
HALF = 4
WAYS = 2
GROUP = HALF * WAYS


def split_hi_lo(x):
    hi = x.astype(jnp.bfloat16)
    lo = (x - hi.astype(jnp.float32)).astype(jnp.bfloat16)
    return hi, lo


def split_mat(x):
    hi = lax.reduce_precision(x, 8, 7)
    return hi.astype(jnp.bfloat16), (x - hi).astype(jnp.bfloat16)


def dot32(a, b):
    return jnp.dot(a, b, preferred_element_type=jnp.float32)


def transport_kernel(
    ends, scal, sum_mat, out_mat, m_c, m_l, m_r, n_c, n_l, n_r, co_c, co_l, co_r,
    halo_l, halo_r, m_out, n_out,
):
    step, steps = pl.program_id(0), pl.num_programs(0)
    chunk = m_c.shape[1]
    first, last = step == 0, step == steps - 1
    rows = CLASSES * SPECIES

    def flat(ref):
        return ref[...].astype(jnp.float32).reshape(rows, ref.shape[2])

    nl = jnp.where(first, halo_l[:rows, :], flat(n_l)).astype(jnp.bfloat16)
    nr = jnp.where(last, halo_r[:rows, :], flat(n_r)).astype(jnp.bfloat16)
    nc = flat(n_c).astype(jnp.bfloat16)
    ml = jnp.where(first, halo_l[rows:rows + SPECIES, :], m_l[...])
    mr = jnp.where(last, halo_r[rows:rows + SPECIES, :], m_r[...])
    cl = jnp.where(first, halo_l[rows + SPECIES:rows + SPECIES + 1, :], co_l[...])
    cr = jnp.where(last, halo_r[rows + SPECIES:rows + SPECIES + 1, :], co_r[...])
    wide = jnp.concatenate([nl, nc, nr], axis=1)
    m = jnp.concatenate([ml, m_c[...], mr], axis=1)
    co = jnp.concatenate([cl, co_c[...], cr], axis=1)
    width = chunk + 2 * EDGE
    lane = lax.broadcasted_iota(jnp.int32, (1, width), 1)
    out_left = (lane < EDGE) & first & (ends[0] == 1)
    out_right = (lane >= EDGE + chunk) & last & (ends[1] == 1)
    valid = jnp.where(out_left | out_right, 0.0, 1.0)
    total = scal[0]
    center_w = (1.0 - co - 2.0 * dispersion - total) * valid
    left_w = (co + dispersion) * valid
    right_w = dispersion * valid
    both = dot32(sum_mat[...], wide)
    sums = both[:TSTEPS * SPECIES] + both[TSTEPS * SPECIES:]
    past = []
    for t in range(TSTEPS):
        past.append(m)
        left = pltpu.roll(m, 1, axis=1)
        right = pltpu.roll(m, width - 1, axis=1)
        extra = sums[t * SPECIES:(t + 1) * SPECIES]
        for j in range(t):
            extra = extra + scal[1 + t - 1 - j] * past[j]
        m = center_w * m + left_w * left + right_w * right + extra * valid
    m_out[...] = m[:, EDGE:EDGE + chunk]
    inner = jnp.concatenate([p[:, EDGE:EDGE + chunk] for p in past], axis=0)
    hi, lo = split_hi_lo(inner)
    stack = jnp.concatenate([nc, nc, hi, hi, lo], axis=0)
    n_new = dot32(out_mat[...], stack)
    n_out[...] = n_new.reshape(CLASSES, SPECIES, chunk).astype(jnp.bfloat16)


def transport(mobile, immobile, courant, exchange_rate, capacity):
    species, length = mobile.shape
    devices = lax.axis_size("slab")
    me = lax.axis_index("slab")
    rows = CLASSES * SPECIES

    def edge(sl):
        return jnp.concatenate(
            [
                immobile[:, :, sl].astype(jnp.float32).reshape(rows, EDGE),
                mobile[:, sl],
                jnp.broadcast_to(courant[None, sl], (8, EDGE)),
            ],
            axis=0,
        )

    up = [(i, i + 1) for i in range(devices - 1)]
    down = [(j, i) for i, j in up]
    halo_l = lax.ppermute(edge(slice(length - EDGE, length)), "slab", up)
    halo_r = lax.ppermute(edge(slice(0, EDGE)), "slab", down)
    ends = jnp.stack([me == 0, me == devices - 1]).astype(jnp.int32)

    x = exchange_rate
    keep = 1.0 - x
    powers = jnp.stack([jnp.ones_like(x), keep, keep * keep, keep * keep * keep])
    cx = capacity * x
    scal = jnp.concatenate([jnp.sum(cx)[None], jnp.sum(cx * x * powers, axis=1)])
    eye = jnp.eye(SPECIES, dtype=jnp.float32)
    sum_mat = ((cx * powers)[:, None, :, None] * eye[None, :, None, :]).reshape(
        TSTEPS * SPECIES, rows
    )
    s_hi, s_lo = split_mat(sum_mat)
    sum_mat = jnp.concatenate([s_hi, s_lo], axis=0)
    own = jnp.eye(CLASSES, dtype=jnp.float32) * (keep * keep * keep * keep)[:, None]
    own = (own[:, None, :, None] * eye[None, :, None, :]).reshape(rows, rows)
    feed = (x * powers[::-1]).T
    feed = (feed[:, None, :, None] * eye[None, :, None, :]).reshape(rows, TSTEPS * SPECIES)
    o_hi, o_lo = split_mat(own)
    f_hi, f_lo = split_mat(feed)
    out_mat = jnp.concatenate([o_hi, o_lo, f_hi, f_lo, f_hi], axis=1)

    chunk = next(c for c in (2048, 1536, 1024, 768, 512, 384, 256, 128) if length % c == 0)
    per = chunk // EDGE
    count = length // EDGE
    steps = length // chunk
    co = courant.reshape(1, length)

    def before(i):
        return jnp.maximum(i * per - 1, 0)

    def after(i):
        return jnp.minimum((i + 1) * per, count - 1)

    smem = pl.BlockSpec(memory_space=pltpu.SMEM)
    whole = lambda a: pl.BlockSpec(a.shape, lambda i: (0,) * a.ndim)
    return pl.pallas_call(
        transport_kernel,
        grid=(steps,),
        out_shape=(
            jax.ShapeDtypeStruct(mobile.shape, jnp.float32),
            jax.ShapeDtypeStruct(immobile.shape, jnp.bfloat16),
        ),
        in_specs=[
            smem,
            smem,
            whole(sum_mat),
            whole(out_mat),
            pl.BlockSpec((species, chunk), lambda i: (0, i)),
            pl.BlockSpec((species, EDGE), lambda i: (0, before(i))),
            pl.BlockSpec((species, EDGE), lambda i: (0, after(i))),
            pl.BlockSpec((CLASSES, species, chunk), lambda i: (0, 0, i)),
            pl.BlockSpec((CLASSES, species, EDGE), lambda i: (0, 0, before(i))),
            pl.BlockSpec((CLASSES, species, EDGE), lambda i: (0, 0, after(i))),
            pl.BlockSpec((1, chunk), lambda i: (0, i)),
            pl.BlockSpec((1, EDGE), lambda i: (0, before(i))),
            pl.BlockSpec((1, EDGE), lambda i: (0, after(i))),
            whole(halo_l),
            whole(halo_r),
        ],
        out_specs=(
            pl.BlockSpec((species, chunk), lambda i: (0, i)),
            pl.BlockSpec((CLASSES, species, chunk), lambda i: (0, 0, i)),
        ),
        compiler_params=pltpu.CompilerParams(vmem_limit_bytes=48 * 2**20),
        name="transport",
    )(
        ends, scal, sum_mat, out_mat, mobile, mobile, mobile, immobile, immobile, immobile,
        co, co, co, halo_l, halo_r,
    )


def substep(concs, qs, mat_full, mat_fast):
    us = list(concs)
    for turn in range(NEWTON):
        lin = []
        for u in us:
            hi, lo = split_hi_lo(u)
            lin.append(dot32(mat_full, jnp.concatenate([hi, lo, hi], axis=0)))
        es, rs = [], []
        for u, c, q, hu in zip(us, concs, qs, lin):
            t = jnp.exp(-jnp.abs(u))
            s = 1.0 + t
            soft = jnp.maximum(u, 0.0) + jnp.log(s)
            if turn == 0:
                r = q * soft - hu
            else:
                r = (u - c) + (q * soft - hu)
            e = s / (s + q * jnp.where(u >= 0.0, 1.0, t))
            es.append(e)
            rs.append(r)
        fast = [dot32(mat_fast, (e * r).astype(jnp.bfloat16)) for e, r in zip(es, rs)]
        us = [u - e * (r + f) for u, e, r, f in zip(us, es, rs, fast)]
    return us


def chem_kernel(kinds, full_l, fast_l, full_h, fast_h, rates, m_ref, mask_ref, out_ref, order):
    count = kinds.shape[0]
    species, length = m_ref.shape
    wide = HALF * BLOCK
    p_light = rates[...] * reaction_step
    p_heavy = rates[...] * (heavy_span / SUBSTEPS)

    def scan(i, n):
        @pl.when(kinds[i] == 1)
        def _():
            order[n] = i
        return n + jnp.where(kinds[i] == 1, 1, 0)

    heavy = lax.fori_loop(0, count, scan, jnp.int32(0))

    @pl.loop(0, length // (wide * WAYS))
    def _(g):
        starts = [pl.multiple_of((g * WAYS + w) * wide, wide) for w in range(WAYS)]
        cs = [m_ref[:, pl.ds(s, wide)] for s in starts]
        qs = [p_light * mask_ref[:, pl.ds(s, wide)].astype(jnp.float32) for s in starts]
        us = substep(cs, qs, full_l[...], fast_l[...])
        for s, u in zip(starts, us):
            out_ref[:, pl.ds(s, wide)] = u

    @pl.loop(0, (heavy + GROUP - 1) // GROUP)
    def _(g):
        picks = [order[jnp.minimum(g * GROUP + j, heavy - 1)] for j in range(GROUP)]
        spots = [pl.ds(pl.multiple_of(b * BLOCK, BLOCK), BLOCK) for b in picks]

        def side(ref, w):
            return jnp.concatenate(
                [ref[:, spots[w * HALF + j]] for j in range(HALF)], axis=1
            )

        cs = [side(m_ref, w) for w in range(WAYS)]
        qs = [p_heavy * side(mask_ref, w).astype(jnp.float32) for w in range(WAYS)]
        done = lax.fori_loop(
            0, SUBSTEPS, lambda i, us: tuple(substep(us, qs, full_h[...], fast_h[...])), tuple(cs)
        )
        for w in range(WAYS):
            for j in range(HALF):
                out_ref[:, spots[w * HALF + j]] = done[w][:, j * BLOCK:(j + 1) * BLOCK]


def chem_mats(reaction):
    base = reaction - jnp.eye(SPECIES, dtype=jnp.float32)
    mats = []
    for h in (reaction_step, heavy_span / SUBSTEPS):
        hi, lo = split_mat(base * h)
        mats += [jnp.concatenate([hi, hi, lo], axis=1), hi]
    return mats


def chemistry(moving, block_class, precip_mask, reaction, precip_rate):
    species, length = moving.shape
    mats = chem_mats(reaction)
    vmem = pl.BlockSpec(memory_space=pltpu.VMEM)
    return pl.pallas_call(
        chem_kernel,
        out_shape=jax.ShapeDtypeStruct(moving.shape, jnp.float32),
        in_specs=[pl.BlockSpec(memory_space=pltpu.SMEM)] + [vmem] * 7,
        out_specs=vmem,
        scratch_shapes=[pltpu.SMEM((block_class.shape[0],), jnp.int32)],
        compiler_params=pltpu.CompilerParams(vmem_limit_bytes=48 * 2**20),
        name="chemistry",
    )(block_class, *mats, precip_rate[:, None], moving, precip_mask.reshape(1, length))


def per_device(
    mobile, immobile, courant, exchange_rate, capacity, reaction, precip_rate, block_class,
    precip_mask,
):
    moving, immobile_out = transport(mobile, immobile, courant, exchange_rate, capacity)
    mobile_out = chemistry(moving, block_class, precip_mask, reaction, precip_rate)
    return (mobile_out, immobile_out)


def solution(mesh):
    in_specs = (
        P(None, ("groups", "slab")),
        P(None, None, ("groups", "slab")),
        P(("groups", "slab")),
        P(),
        P(),
        P(),
        P(),
        P(("groups", "slab")),
        P(("groups", "slab")),
    )
    out_specs = (P(None, ("groups", "slab")), P(None, None, ("groups", "slab")))
    return jax.shard_map(
        per_device, mesh=mesh, in_specs=in_specs, out_specs=out_specs, check_vma=False
    )
```

```python
from functools import partial

import jax
import jax.numpy as jnp
from jax import lax
from jax.experimental import pallas as pl
from jax.experimental.pallas import tpu as pltpu
from jax.sharding import PartitionSpec as P

BLOCK = 128
TSTEPS = 4
NEWTON = 3
SUBSTEPS = 20

dispersion = 0.05
reaction_step = 0.25
heavy_span = 4.0

EDGE = 128
LOG2E = 1.4426950408889634
LN2 = 0.6931471805599453
CLASSES = 8
SPECIES = 24
GROUP = 32


def split_hi_lo(x):
    hi = x.astype(jnp.bfloat16)
    lo = (x - hi.astype(jnp.float32)).astype(jnp.bfloat16)
    return hi, lo


def split_mat(x):
    hi = lax.reduce_precision(x, 8, 7)
    return hi.astype(jnp.bfloat16), (x - hi).astype(jnp.bfloat16)


def dot32(a, b):
    return jnp.dot(a, b, preferred_element_type=jnp.float32)


def transport_kernel(
    ends, scal, sum_mat, out_mat, m_c, m_l, m_r, n_c, n_l, n_r, co_c, co_l, co_r,
    halo_l, halo_r, m_out, n_out,
):
    step, steps = pl.program_id(0), pl.num_programs(0)
    chunk = m_c.shape[1]
    first, last = step == 0, step == steps - 1
    rows = CLASSES * SPECIES

    def flat(ref):
        return ref[...].astype(jnp.float32).reshape(rows, ref.shape[2])

    nl = jnp.where(first, halo_l[:rows, :], flat(n_l)).astype(jnp.bfloat16)
    nr = jnp.where(last, halo_r[:rows, :], flat(n_r)).astype(jnp.bfloat16)
    nc = flat(n_c).astype(jnp.bfloat16)
    ml = jnp.where(first, halo_l[rows:rows + SPECIES, :], m_l[...])
    mr = jnp.where(last, halo_r[rows:rows + SPECIES, :], m_r[...])
    cl = jnp.where(first, halo_l[rows + SPECIES:rows + SPECIES + 1, :], co_l[...])
    cr = jnp.where(last, halo_r[rows + SPECIES:rows + SPECIES + 1, :], co_r[...])
    wide = jnp.concatenate([nl, nc, nr], axis=1)
    m = jnp.concatenate([ml, m_c[...], mr], axis=1)
    co = jnp.concatenate([cl, co_c[...], cr], axis=1)
    width = chunk + 2 * EDGE
    lane = lax.broadcasted_iota(jnp.int32, (1, width), 1)
    out_left = (lane < EDGE) & first & (ends[0] == 1)
    out_right = (lane >= EDGE + chunk) & last & (ends[1] == 1)
    valid = jnp.where(out_left | out_right, 0.0, 1.0)
    total = scal[0]
    center_w = (1.0 - co - 2.0 * dispersion - total) * valid
    left_w = (co + dispersion) * valid
    right_w = dispersion * valid
    both = dot32(sum_mat[...], wide)
    sums = both[:TSTEPS * SPECIES] + both[TSTEPS * SPECIES:]
    past = []
    for t in range(TSTEPS):
        past.append(m)
        left = pltpu.roll(m, 1, axis=1)
        right = pltpu.roll(m, width - 1, axis=1)
        extra = sums[t * SPECIES:(t + 1) * SPECIES]
        for j in range(t):
            extra = extra + scal[1 + t - 1 - j] * past[j]
        m = center_w * m + left_w * left + right_w * right + extra * valid
    m_out[...] = m[:, EDGE:EDGE + chunk]
    inner = jnp.concatenate([p[:, EDGE:EDGE + chunk] for p in past], axis=0)
    hi, lo = split_hi_lo(inner)
    stack = jnp.concatenate([nc, nc, hi, hi, lo], axis=0)
    n_new = dot32(out_mat[...], stack)
    n_out[...] = n_new.reshape(CLASSES, SPECIES, chunk).astype(jnp.bfloat16)


def transport(mobile, immobile, courant, exchange_rate, capacity):
    species, length = mobile.shape
    devices = lax.axis_size("slab")
    me = lax.axis_index("slab")
    rows = CLASSES * SPECIES

    def edge(sl):
        return jnp.concatenate(
            [
                immobile[:, :, sl].astype(jnp.float32).reshape(rows, EDGE),
                mobile[:, sl],
                jnp.broadcast_to(courant[None, sl], (8, EDGE)),
            ],
            axis=0,
        )

    up = [(i, i + 1) for i in range(devices - 1)]
    down = [(j, i) for i, j in up]
    halo_l = lax.ppermute(edge(slice(length - EDGE, length)), "slab", up)
    halo_r = lax.ppermute(edge(slice(0, EDGE)), "slab", down)
    ends = jnp.stack([me == 0, me == devices - 1]).astype(jnp.int32)

    x = exchange_rate
    keep = 1.0 - x
    powers = jnp.stack([jnp.ones_like(x), keep, keep * keep, keep * keep * keep])
    cx = capacity * x
    scal = jnp.concatenate([jnp.sum(cx)[None], jnp.sum(cx * x * powers, axis=1)])
    eye = jnp.eye(SPECIES, dtype=jnp.float32)
    sum_mat = ((cx * powers)[:, None, :, None] * eye[None, :, None, :]).reshape(
        TSTEPS * SPECIES, rows
    )
    s_hi, s_lo = split_mat(sum_mat)
    sum_mat = jnp.concatenate([s_hi, s_lo], axis=0)
    own = jnp.eye(CLASSES, dtype=jnp.float32) * (keep * keep * keep * keep)[:, None]
    own = (own[:, None, :, None] * eye[None, :, None, :]).reshape(rows, rows)
    feed = (x * powers[::-1]).T
    feed = (feed[:, None, :, None] * eye[None, :, None, :]).reshape(rows, TSTEPS * SPECIES)
    o_hi, o_lo = split_mat(own)
    f_hi, f_lo = split_mat(feed)
    out_mat = jnp.concatenate([o_hi, o_lo, f_hi, f_lo, f_hi], axis=1)

    chunk = next(c for c in (2048, 1536, 1024, 768, 512, 384, 256, 128) if length % c == 0)
    per = chunk // EDGE
    count = length // EDGE
    steps = length // chunk
    co = courant.reshape(1, length)

    def before(i):
        return jnp.maximum(i * per - 1, 0)

    def after(i):
        return jnp.minimum((i + 1) * per, count - 1)

    smem = pl.BlockSpec(memory_space=pltpu.SMEM)
    whole = lambda a: pl.BlockSpec(a.shape, lambda i: (0,) * a.ndim)
    return pl.pallas_call(
        transport_kernel,
        grid=(steps,),
        out_shape=(
            jax.ShapeDtypeStruct(mobile.shape, jnp.float32),
            jax.ShapeDtypeStruct(immobile.shape, jnp.bfloat16),
        ),
        in_specs=[
            smem,
            smem,
            whole(sum_mat),
            whole(out_mat),
            pl.BlockSpec((species, chunk), lambda i: (0, i)),
            pl.BlockSpec((species, EDGE), lambda i: (0, before(i))),
            pl.BlockSpec((species, EDGE), lambda i: (0, after(i))),
            pl.BlockSpec((CLASSES, species, chunk), lambda i: (0, 0, i)),
            pl.BlockSpec((CLASSES, species, EDGE), lambda i: (0, 0, before(i))),
            pl.BlockSpec((CLASSES, species, EDGE), lambda i: (0, 0, after(i))),
            pl.BlockSpec((1, chunk), lambda i: (0, i)),
            pl.BlockSpec((1, EDGE), lambda i: (0, before(i))),
            pl.BlockSpec((1, EDGE), lambda i: (0, after(i))),
            whole(halo_l),
            whole(halo_r),
        ],
        out_specs=(
            pl.BlockSpec((species, chunk), lambda i: (0, i)),
            pl.BlockSpec((CLASSES, species, chunk), lambda i: (0, 0, i)),
        ),
        compiler_params=pltpu.CompilerParams(vmem_limit_bytes=48 * 2**20),
        name="transport",
    )(
        ends, scal, sum_mat, out_mat, mobile, mobile, mobile, immobile, immobile, immobile,
        co, co, co, halo_l, halo_r,
    )


def substep(concs, qs, mat_full, mat_fast):
    us = list(concs)
    for turn in range(NEWTON):
        lin = []
        for u in us:
            hi = u.astype(jnp.bfloat16).astype(jnp.float32)
            lin.append(dot32(mat_full, jnp.concatenate([hi, u - hi, hi], axis=0).astype(jnp.bfloat16)))
        es, rs = [], []
        for u, c, q, hu in zip(us, concs, qs, lin):
            t = jnp.exp2(-jnp.abs(u))
            s = 1.0 + t
            soft = jnp.maximum(u, 0.0) + jnp.log2(s)
            if turn == 0:
                r = q * soft - hu
            else:
                r = (u - c) + (q * soft - hu)
            e = s * pl.reciprocal(s + q * jnp.where(u >= 0.0, 1.0, t), approx=True)
            es.append(e)
            rs.append(r)
        fast = [dot32(mat_fast, (e * r).astype(jnp.bfloat16)) for e, r in zip(es, rs)]
        us = [u - e * (r + f) for u, e, r, f in zip(us, es, rs, fast)]
    return us


def chem_kernel(kinds, full_l, fast_l, full_h, fast_h, rates, m_ref, mask_ref, out_ref, order):
    count = kinds.shape[0]
    species, length = m_ref.shape
    p_light = rates[...] * reaction_step
    p_heavy = rates[...] * (heavy_span / SUBSTEPS)

    def scan(i, n):
        @pl.when(kinds[i] == 1)
        def _():
            order[n] = i
        return n + jnp.where(kinds[i] == 1, 1, 0)

    heavy = lax.fori_loop(0, count, scan, jnp.int32(0))

    chunk = next(c for c in (32, 24, 16, 12, 8, 6, 4, 3, 2, 1) if count % c == 0)
    parts = ways_of(chunk)

    @pl.loop(0, count // chunk)
    def _(g):
        starts, at = [], 0
        for width in parts:
            starts.append((pl.multiple_of((g * chunk + at) * BLOCK, BLOCK), width * BLOCK))
            at += width
        cs = [m_ref[:, pl.ds(s, w)] * LOG2E for s, w in starts]
        qs = [p_light * mask_ref[:, pl.ds(s, w)].astype(jnp.float32) for s, w in starts]
        us = substep(cs, qs, full_l[...], fast_l[...])
        for (s, w), u in zip(starts, us):
            out_ref[:, pl.ds(s, w)] = u * LN2

    def run(base, size):
        widths = ways_of(size)
        picks = [order[jnp.minimum(base + j, heavy - 1)] for j in range(size)]
        spots = [pl.ds(pl.multiple_of(b * BLOCK, BLOCK), BLOCK) for b in picks]
        sides, at = [], 0
        for width in widths:
            sides.append(spots[at:at + width])
            at += width

        def side(ref, places):
            return jnp.concatenate([ref[:, p] for p in places], axis=1)

        cs = [side(m_ref, p) * LOG2E for p in sides]
        qs = [p_heavy * side(mask_ref, p).astype(jnp.float32) for p in sides]
        done = lax.fori_loop(
            0, SUBSTEPS, lambda i, us: tuple(substep(us, qs, full_h[...], fast_h[...])), tuple(cs)
        )
        for p, u in zip(sides, done):
            for j, place in enumerate(p):
                out_ref[:, place] = u[:, j * BLOCK:(j + 1) * BLOCK] * LN2

    fulls = heavy // GROUP

    @pl.loop(0, fulls)
    def _(g):
        run(g * GROUP, GROUP)

    rest = heavy - fulls * GROUP
    for least, size in ((0, 8), (8, 16), (16, 24), (24, 32)):
        @pl.when((rest > least) & (rest <= size))
        def _(size=size):
            run(fulls * GROUP, size)


def ways_of(size):
    step = 8
    return [min(step, size - at) for at in range(0, size, step)]


def chem_mats(reaction):
    base = reaction - jnp.eye(SPECIES, dtype=jnp.float32)
    mats = []
    for h in (reaction_step, heavy_span / SUBSTEPS):
        hi, lo = split_mat(base * h)
        mats += [jnp.concatenate([hi, hi, lo], axis=1), hi]
    return mats


def chemistry(moving, block_class, precip_mask, reaction, precip_rate):
    species, length = moving.shape
    mats = chem_mats(reaction)
    vmem = pl.BlockSpec(memory_space=pltpu.VMEM)
    return pl.pallas_call(
        chem_kernel,
        out_shape=jax.ShapeDtypeStruct(moving.shape, jnp.float32),
        in_specs=[pl.BlockSpec(memory_space=pltpu.SMEM)] + [vmem] * 7,
        out_specs=vmem,
        scratch_shapes=[pltpu.SMEM((block_class.shape[0],), jnp.int32)],
        compiler_params=pltpu.CompilerParams(vmem_limit_bytes=48 * 2**20),
        name="chemistry",
    )(block_class, *mats, precip_rate[:, None], moving, precip_mask.reshape(1, length))


def per_device(
    mobile, immobile, courant, exchange_rate, capacity, reaction, precip_rate, block_class,
    precip_mask,
):
    moving, immobile_out = transport(mobile, immobile, courant, exchange_rate, capacity)
    mobile_out = chemistry(moving, block_class, precip_mask, reaction, precip_rate)
    return (mobile_out, immobile_out)


def solution(mesh):
    in_specs = (
        P(None, ("groups", "slab")),
        P(None, None, ("groups", "slab")),
        P(("groups", "slab")),
        P(),
        P(),
        P(),
        P(),
        P(("groups", "slab")),
        P(("groups", "slab")),
    )
    out_specs = (P(None, ("groups", "slab")), P(None, None, ("groups", "slab")))
    return jax.shard_map(
        per_device, mesh=mesh, in_specs=in_specs, out_specs=out_specs, check_vma=False
    )
```

```python
from functools import partial

import jax
import jax.numpy as jnp
from jax import lax
from jax.experimental import pallas as pl
from jax.experimental.pallas import tpu as pltpu
from jax.sharding import PartitionSpec as P

BLOCK = 128
TSTEPS = 4
NEWTON = 3
SUBSTEPS = 20

dispersion = 0.05
reaction_step = 0.25
heavy_span = 4.0

EDGE = 128
LOG2E = 1.4426950408889634
LN2 = 0.6931471805599453
CLASSES = 8
SPECIES = 24
GROUP = 32
PEERS = 3


def split_hi_lo(x):
    hi = x.astype(jnp.bfloat16)
    lo = (x - hi.astype(jnp.float32)).astype(jnp.bfloat16)
    return hi, lo


def split_mat(x):
    hi = lax.reduce_precision(x, 8, 7)
    return hi.astype(jnp.bfloat16), (x - hi).astype(jnp.bfloat16)


def dot32(a, b):
    return jnp.dot(a, b, preferred_element_type=jnp.float32)


def transport_kernel(
    ends, scal, sum_mat, out_mat, m_c, m_l, m_r, n_c, n_l, n_r, co_c, co_l, co_r,
    halo_l, halo_r, m_out, n_out,
):
    step, steps = pl.program_id(0), pl.num_programs(0)
    chunk = m_c.shape[1]
    first, last = step == 0, step == steps - 1
    rows = CLASSES * SPECIES

    def flat(ref):
        return ref[...].astype(jnp.float32).reshape(rows, ref.shape[2])

    nl = jnp.where(first, halo_l[:rows, :], flat(n_l)).astype(jnp.bfloat16)
    nr = jnp.where(last, halo_r[:rows, :], flat(n_r)).astype(jnp.bfloat16)
    nc = flat(n_c).astype(jnp.bfloat16)
    ml = jnp.where(first, halo_l[rows:rows + SPECIES, :], m_l[...])
    mr = jnp.where(last, halo_r[rows:rows + SPECIES, :], m_r[...])
    cl = jnp.where(first, halo_l[rows + SPECIES:rows + SPECIES + 1, :], co_l[...])
    cr = jnp.where(last, halo_r[rows + SPECIES:rows + SPECIES + 1, :], co_r[...])
    wide = jnp.concatenate([nl, nc, nr], axis=1)
    m = jnp.concatenate([ml, m_c[...], mr], axis=1)
    co = jnp.concatenate([cl, co_c[...], cr], axis=1)
    width = chunk + 2 * EDGE
    lane = lax.broadcasted_iota(jnp.int32, (1, width), 1)
    out_left = (lane < EDGE) & first & (ends[0] == 1)
    out_right = (lane >= EDGE + chunk) & last & (ends[1] == 1)
    valid = jnp.where(out_left | out_right, 0.0, 1.0)
    total = scal[0]
    center_w = (1.0 - co - 2.0 * dispersion - total) * valid
    left_w = (co + dispersion) * valid
    right_w = dispersion * valid
    both = dot32(sum_mat[...], wide)
    sums = both[:TSTEPS * SPECIES] + both[TSTEPS * SPECIES:]
    past = []
    for t in range(TSTEPS):
        past.append(m)
        left = pltpu.roll(m, 1, axis=1)
        right = pltpu.roll(m, width - 1, axis=1)
        extra = sums[t * SPECIES:(t + 1) * SPECIES]
        for j in range(t):
            extra = extra + scal[1 + t - 1 - j] * past[j]
        m = center_w * m + left_w * left + right_w * right + extra * valid
    m_out[...] = m[:, EDGE:EDGE + chunk]
    inner = jnp.concatenate([p[:, EDGE:EDGE + chunk] for p in past], axis=0)
    hi, lo = split_hi_lo(inner)
    stack = jnp.concatenate([nc, nc, hi, hi, lo], axis=0)
    n_new = dot32(out_mat[...], stack)
    n_out[...] = n_new.reshape(CLASSES, SPECIES, chunk).astype(jnp.bfloat16)


def transport(mobile, immobile, courant, exchange_rate, capacity):
    species, length = mobile.shape
    devices = lax.axis_size("slab")
    me = lax.axis_index("slab")
    rows = CLASSES * SPECIES

    def edge(sl):
        return jnp.concatenate(
            [
                immobile[:, :, sl].astype(jnp.float32).reshape(rows, EDGE),
                mobile[:, sl],
                jnp.broadcast_to(courant[None, sl], (8, EDGE)),
            ],
            axis=0,
        )

    up = [(i, i + 1) for i in range(devices - 1)]
    down = [(j, i) for i, j in up]
    halo_l = lax.ppermute(edge(slice(length - EDGE, length)), "slab", up)
    halo_r = lax.ppermute(edge(slice(0, EDGE)), "slab", down)
    ends = jnp.stack([me == 0, me == devices - 1]).astype(jnp.int32)

    x = exchange_rate
    keep = 1.0 - x
    powers = jnp.stack([jnp.ones_like(x), keep, keep * keep, keep * keep * keep])
    cx = capacity * x
    scal = jnp.concatenate([jnp.sum(cx)[None], jnp.sum(cx * x * powers, axis=1)])
    eye = jnp.eye(SPECIES, dtype=jnp.float32)
    sum_mat = ((cx * powers)[:, None, :, None] * eye[None, :, None, :]).reshape(
        TSTEPS * SPECIES, rows
    )
    s_hi, s_lo = split_mat(sum_mat)
    sum_mat = jnp.concatenate([s_hi, s_lo], axis=0)
    own = jnp.eye(CLASSES, dtype=jnp.float32) * (keep * keep * keep * keep)[:, None]
    own = (own[:, None, :, None] * eye[None, :, None, :]).reshape(rows, rows)
    feed = (x * powers[::-1]).T
    feed = (feed[:, None, :, None] * eye[None, :, None, :]).reshape(rows, TSTEPS * SPECIES)
    o_hi, o_lo = split_mat(own)
    f_hi, f_lo = split_mat(feed)
    out_mat = jnp.concatenate([o_hi, o_lo, f_hi, f_lo, f_hi], axis=1)

    chunk = next(c for c in (2048, 1536, 1024, 768, 512, 384, 256, 128) if length % c == 0)
    per = chunk // EDGE
    count = length // EDGE
    steps = length // chunk
    co = courant.reshape(1, length)

    def before(i):
        return jnp.maximum(i * per - 1, 0)

    def after(i):
        return jnp.minimum((i + 1) * per, count - 1)

    smem = pl.BlockSpec(memory_space=pltpu.SMEM)
    whole = lambda a: pl.BlockSpec(a.shape, lambda i: (0,) * a.ndim)
    return pl.pallas_call(
        transport_kernel,
        grid=(steps,),
        out_shape=(
            jax.ShapeDtypeStruct(mobile.shape, jnp.float32),
            jax.ShapeDtypeStruct(immobile.shape, jnp.bfloat16),
        ),
        in_specs=[
            smem,
            smem,
            whole(sum_mat),
            whole(out_mat),
            pl.BlockSpec((species, chunk), lambda i: (0, i)),
            pl.BlockSpec((species, EDGE), lambda i: (0, before(i))),
            pl.BlockSpec((species, EDGE), lambda i: (0, after(i))),
            pl.BlockSpec((CLASSES, species, chunk), lambda i: (0, 0, i)),
            pl.BlockSpec((CLASSES, species, EDGE), lambda i: (0, 0, before(i))),
            pl.BlockSpec((CLASSES, species, EDGE), lambda i: (0, 0, after(i))),
            pl.BlockSpec((1, chunk), lambda i: (0, i)),
            pl.BlockSpec((1, EDGE), lambda i: (0, before(i))),
            pl.BlockSpec((1, EDGE), lambda i: (0, after(i))),
            whole(halo_l),
            whole(halo_r),
        ],
        out_specs=(
            pl.BlockSpec((species, chunk), lambda i: (0, i)),
            pl.BlockSpec((CLASSES, species, chunk), lambda i: (0, 0, i)),
        ),
        compiler_params=pltpu.CompilerParams(vmem_limit_bytes=48 * 2**20),
        name="transport",
    )(
        ends, scal, sum_mat, out_mat, mobile, mobile, mobile, immobile, immobile, immobile,
        co, co, co, halo_l, halo_r,
    )


def substep(concs, qs, mat_full, mat_fast):
    us = list(concs)
    for turn in range(NEWTON):
        lin = []
        for u in us:
            hi = u.astype(jnp.bfloat16).astype(jnp.float32)
            lin.append(dot32(mat_full, jnp.concatenate([hi, u - hi, hi], axis=0).astype(jnp.bfloat16)))
        es, rs = [], []
        for u, c, q, hu in zip(us, concs, qs, lin):
            t = jnp.exp2(-jnp.abs(u))
            s = 1.0 + t
            soft = jnp.maximum(u, 0.0) + jnp.log2(s)
            if turn == 0:
                r = q * soft - hu
            else:
                r = (u - c) + (q * soft - hu)
            e = s * pl.reciprocal(s + q * jnp.where(u >= 0.0, 1.0, t), approx=True)
            es.append(e)
            rs.append(r)
        fast = [dot32(mat_fast, (e * r).astype(jnp.bfloat16)) for e, r in zip(es, rs)]
        us = [u - e * (r + f) for u, e, r, f in zip(us, es, rs, fast)]
    return us


def scan_heavy(kinds, order):
    def scan(i, n):
        @pl.when(kinds[i] == 1)
        def _():
            order[n] = i
        return n + jnp.where(kinds[i] == 1, 1, 0)

    return lax.fori_loop(0, kinds.shape[0], scan, jnp.int32(0))


def spot(index):
    return pl.ds(pl.multiple_of(index * BLOCK, BLOCK), BLOCK)


def share_of(heavy, peer):
    return (heavy + PEERS - peer) // (PEERS + 1)


def pack_kernel(kinds, m_ref, mask_ref, *rest):
    outs, order = rest[:PEERS], rest[PEERS]
    heavy = scan_heavy(kinds, order)
    for peer, out in enumerate(outs, 1):
        n = share_of(heavy, peer)
        depth = out.shape[1] // BLOCK - 2
        out[...] = jnp.zeros_like(out)
        out[:, (depth + 1) * BLOCK:] = jnp.full((SPECIES, BLOCK), n, jnp.int32).astype(jnp.float32)

        @pl.loop(0, n)
        def _(j):
            b = order[j * (PEERS + 1) + peer]
            out[:, spot(j)] = m_ref[:, spot(b)]
            row = lax.broadcasted_iota(jnp.int32, (SPECIES, BLOCK), 0) == j
            masks = jnp.broadcast_to(mask_ref[:, spot(b)].astype(jnp.float32), (SPECIES, BLOCK))
            kept = out[:, depth * BLOCK:(depth + 1) * BLOCK]
            out[:, depth * BLOCK:(depth + 1) * BLOCK] = jnp.where(row, masks, kept)


def react_list(count, pick, src, mask, dst, full, fast, rates):
    def run(base, size):
        widths = ways_of(size)
        spots = [spot(pick(jnp.minimum(base + j, count - 1))) for j in range(size)]
        sides, at = [], 0
        for width in widths:
            sides.append(spots[at:at + width])
            at += width

        def side(ref, places):
            return jnp.concatenate([ref[:, p] for p in places], axis=1)

        cs = [side(src, p) * LOG2E for p in sides]
        qs = [rates * side(mask, p).astype(jnp.float32) for p in sides]
        done = lax.fori_loop(
            0, SUBSTEPS, lambda i, us: tuple(substep(us, qs, full[...], fast[...])), tuple(cs)
        )
        for p, u in zip(sides, done):
            for j, place in enumerate(p):
                dst[:, place] = u[:, j * BLOCK:(j + 1) * BLOCK] * LN2

    fulls = count // GROUP

    @pl.loop(0, fulls)
    def _(g):
        run(g * GROUP, GROUP)

    rest = count - fulls * GROUP
    for least, size in ((0, 8), (8, 16), (16, 24), (24, 32)):
        @pl.when((rest > least) & (rest <= size))
        def _(size=size):
            run(fulls * GROUP, size)


def own_kernel(kinds, full_l, fast_l, full_h, fast_h, rates, m_ref, mask_ref, out_ref, order):
    count = kinds.shape[0]
    p_light = rates[...] * reaction_step
    p_heavy = rates[...] * (heavy_span / SUBSTEPS)
    heavy = scan_heavy(kinds, order)
    chunk = next(c for c in (32, 24, 16, 12, 8, 6, 4, 3, 2, 1) if count % c == 0)
    parts = ways_of(chunk)

    @pl.loop(0, count // chunk)
    def _(g):
        starts, at = [], 0
        for width in parts:
            starts.append((pl.multiple_of((g * chunk + at) * BLOCK, BLOCK), width * BLOCK))
            at += width
        cs = [m_ref[:, pl.ds(s, w)] * LOG2E for s, w in starts]
        qs = [p_light * mask_ref[:, pl.ds(s, w)].astype(jnp.float32) for s, w in starts]
        us = substep(cs, qs, full_l[...], fast_l[...])
        for (s, w), u in zip(starts, us):
            out_ref[:, pl.ds(s, w)] = u * LN2

    react_list(
        share_of(heavy, 0), lambda j: order[j * (PEERS + 1)], m_ref, mask_ref, out_ref, full_h,
        fast_h, p_heavy,
    )


def guest_kernel(full_h, fast_h, rates, *rest):
    ins, outs = rest[:PEERS], rest[PEERS:2 * PEERS]
    conc, mask = rest[2 * PEERS:]
    p_heavy = rates[...] * (heavy_span / SUBSTEPS)
    depth = outs[0].shape[1] // BLOCK
    counts = [
        jnp.max(r[0:1, (depth + 1) * BLOCK:(depth + 2) * BLOCK]).astype(jnp.int32) for r in ins
    ]
    bases, total = [], jnp.int32(0)
    for n in counts:
        bases.append(total)
        total = total + n
    for ref, n, base in zip(ins, counts, bases):
        @pl.loop(0, n)
        def _(j, ref=ref, base=base):
            conc[:, spot(base + j)] = ref[:, spot(j)]
            row = lax.broadcasted_iota(jnp.int32, (SPECIES, BLOCK), 0) == j
            masks = jnp.where(row, ref[:, depth * BLOCK:(depth + 1) * BLOCK], 0.0)
            mask[:, spot(base + j)] = jnp.sum(masks, axis=0, keepdims=True)
    react_list(total, lambda j: j, conc, mask, conc, full_h, fast_h, p_heavy)
    for ref, n, base in zip(outs, counts, bases):
        ref[...] = jnp.zeros_like(ref)

        @pl.loop(0, n)
        def _(j, ref=ref, base=base):
            ref[:, spot(j)] = conc[:, spot(base + j)]


def merge_kernel(kinds, own_ref, *rest):
    backs, out_ref, order = rest[:PEERS], rest[PEERS], rest[PEERS + 1]
    heavy = scan_heavy(kinds, order)
    out_ref[...] = own_ref[...]
    for peer, back in enumerate(backs, 1):
        @pl.loop(0, share_of(heavy, peer))
        def _(j, peer=peer, back=back):
            out_ref[:, spot(order[j * (PEERS + 1) + peer])] = back[:, spot(j)]


def ways_of(size):
    step = 8
    return [min(step, size - at) for at in range(0, size, step)]


def chem_mats(reaction):
    base = reaction - jnp.eye(SPECIES, dtype=jnp.float32)
    mats = []
    for h in (reaction_step, heavy_span / SUBSTEPS):
        hi, lo = split_mat(base * h)
        mats += [jnp.concatenate([hi, hi, lo], axis=1), hi]
    return mats


def chemistry(moving, block_class, precip_mask, reaction, precip_rate):
    species, length = moving.shape
    count = block_class.shape[0]
    devices = lax.axis_size("slab")
    depth = -(-count // (PEERS + 1))
    full_l, fast_l, full_h, fast_h = chem_mats(reaction)
    rates = precip_rate[:, None]
    mask = precip_mask.reshape(1, length)
    vmem = pl.BlockSpec(memory_space=pltpu.VMEM)
    smem = pl.BlockSpec(memory_space=pltpu.SMEM)
    order = pltpu.SMEM((count,), jnp.int32)
    params = pltpu.CompilerParams(vmem_limit_bytes=40 * 2**20)
    packed = jax.ShapeDtypeStruct((species, (depth + 2) * BLOCK), jnp.float32)
    slots = jax.ShapeDtypeStruct((species, depth * BLOCK), jnp.float32)
    whole = jax.ShapeDtypeStruct(moving.shape, jnp.float32)
    swaps = [[(i, i ^ bit) for i in range(devices)] for bit in (1, 2, 4)[:PEERS]]

    sent = pl.pallas_call(
        pack_kernel,
        out_shape=(packed,) * PEERS,
        in_specs=[smem, vmem, vmem],
        out_specs=(vmem,) * PEERS,
        scratch_shapes=[order],
        compiler_params=params,
        name="pack",
    )(block_class, moving, mask)
    guests = [lax.ppermute(x, "slab", swap) for x, swap in zip(sent, swaps)]
    own = pl.pallas_call(
        own_kernel,
        out_shape=whole,
        in_specs=[smem] + [vmem] * 7,
        out_specs=vmem,
        scratch_shapes=[order],
        compiler_params=params,
        cost_estimate=pl.CostEstimate(
            flops=10**10, bytes_accessed=8 * species * length, transcendentals=10**8
        ),
        name="own_blocks",
    )(block_class, full_l, fast_l, full_h, fast_h, rates, moving, mask)
    reacted = pl.pallas_call(
        guest_kernel,
        out_shape=(slots,) * PEERS,
        in_specs=[vmem] * (3 + PEERS),
        out_specs=(vmem,) * PEERS,
        scratch_shapes=[
            pltpu.VMEM((species, PEERS * depth * BLOCK), jnp.float32),
            pltpu.VMEM((1, PEERS * depth * BLOCK), jnp.float32),
        ],
        compiler_params=params,
        name="guest_blocks",
    )(full_h, fast_h, rates, *guests)
    backs = [lax.ppermute(x, "slab", swap) for x, swap in zip(reacted, swaps)]
    return pl.pallas_call(
        merge_kernel,
        out_shape=whole,
        in_specs=[smem] + [vmem] * (1 + PEERS),
        out_specs=vmem,
        scratch_shapes=[order],
        compiler_params=params,
        name="merge",
    )(block_class, own, *backs)


def per_device(
    mobile, immobile, courant, exchange_rate, capacity, reaction, precip_rate, block_class,
    precip_mask,
):
    moving, immobile_out = transport(mobile, immobile, courant, exchange_rate, capacity)
    mobile_out = chemistry(moving, block_class, precip_mask, reaction, precip_rate)
    return (mobile_out, immobile_out)


def solution(mesh):
    in_specs = (
        P(None, ("groups", "slab")),
        P(None, None, ("groups", "slab")),
        P(("groups", "slab")),
        P(),
        P(),
        P(),
        P(),
        P(("groups", "slab")),
        P(("groups", "slab")),
    )
    out_specs = (P(None, ("groups", "slab")), P(None, None, ("groups", "slab")))
    return jax.shard_map(
        per_device, mesh=mesh, in_specs=in_specs, out_specs=out_specs, check_vma=False
    )
```

```python
from functools import partial

import jax
import jax.numpy as jnp
from jax import lax
from jax.experimental import pallas as pl
from jax.experimental.pallas import tpu as pltpu
from jax.sharding import PartitionSpec as P

BLOCK = 128
TSTEPS = 4
NEWTON = 3
SUBSTEPS = 20

dispersion = 0.05
reaction_step = 0.25
heavy_span = 4.0

EDGE = 128
LOG2E = 1.4426950408889634
LN2 = 0.6931471805599453
CLASSES = 8
SPECIES = 24
GROUP = 32
PEERS = 3


def split_hi_lo(x):
    hi = x.astype(jnp.bfloat16)
    lo = (x - hi.astype(jnp.float32)).astype(jnp.bfloat16)
    return hi, lo


def split_mat(x):
    hi = lax.reduce_precision(x, 8, 7)
    return hi.astype(jnp.bfloat16), (x - hi).astype(jnp.bfloat16)


def dot32(a, b):
    return jnp.dot(a, b, preferred_element_type=jnp.float32)


def transport_kernel(
    ends, scal, sum_mat, out_mat, m_c, m_l, m_r, n_c, n_l, n_r, co_c, co_l, co_r,
    halo_l, halo_r, m_out, n_out,
):
    step, steps = pl.program_id(0), pl.num_programs(0)
    chunk = m_c.shape[1]
    first, last = step == 0, step == steps - 1
    rows = CLASSES * SPECIES

    def flat(ref):
        return ref[...].astype(jnp.float32).reshape(rows, ref.shape[2])

    nl = jnp.where(first, halo_l[:rows, :], flat(n_l)).astype(jnp.bfloat16)
    nr = jnp.where(last, halo_r[:rows, :], flat(n_r)).astype(jnp.bfloat16)
    nc = flat(n_c).astype(jnp.bfloat16)
    ml = jnp.where(first, halo_l[rows:rows + SPECIES, :], m_l[...])
    mr = jnp.where(last, halo_r[rows:rows + SPECIES, :], m_r[...])
    cl = jnp.where(first, halo_l[rows + SPECIES:rows + SPECIES + 1, :], co_l[...])
    cr = jnp.where(last, halo_r[rows + SPECIES:rows + SPECIES + 1, :], co_r[...])
    wide = jnp.concatenate([nl, nc, nr], axis=1)
    m = jnp.concatenate([ml, m_c[...], mr], axis=1)
    co = jnp.concatenate([cl, co_c[...], cr], axis=1)
    width = chunk + 2 * EDGE
    lane = lax.broadcasted_iota(jnp.int32, (1, width), 1)
    out_left = (lane < EDGE) & first & (ends[0] == 1)
    out_right = (lane >= EDGE + chunk) & last & (ends[1] == 1)
    valid = jnp.where(out_left | out_right, 0.0, 1.0)
    total = scal[0]
    center_w = (1.0 - co - 2.0 * dispersion - total) * valid
    left_w = (co + dispersion) * valid
    right_w = dispersion * valid
    both = dot32(sum_mat[...], wide)
    sums = both[:TSTEPS * SPECIES] + both[TSTEPS * SPECIES:]
    past = []
    for t in range(TSTEPS):
        past.append(m)
        left = pltpu.roll(m, 1, axis=1)
        right = pltpu.roll(m, width - 1, axis=1)
        extra = sums[t * SPECIES:(t + 1) * SPECIES]
        for j in range(t):
            extra = extra + scal[1 + t - 1 - j] * past[j]
        m = center_w * m + left_w * left + right_w * right + extra * valid
    m_out[...] = m[:, EDGE:EDGE + chunk]
    inner = jnp.concatenate([p[:, EDGE:EDGE + chunk] for p in past], axis=0)
    hi, lo = split_hi_lo(inner)
    stack = jnp.concatenate([nc, nc, hi, hi, lo], axis=0)
    n_new = dot32(out_mat[...], stack)
    n_out[...] = n_new.reshape(CLASSES, SPECIES, chunk).astype(jnp.bfloat16)


def transport(mobile, immobile, courant, exchange_rate, capacity):
    species, length = mobile.shape
    devices = lax.axis_size("slab")
    me = lax.axis_index("slab")
    rows = CLASSES * SPECIES

    def edge(sl):
        return jnp.concatenate(
            [
                immobile[:, :, sl].astype(jnp.float32).reshape(rows, EDGE),
                mobile[:, sl],
                jnp.broadcast_to(courant[None, sl], (8, EDGE)),
            ],
            axis=0,
        )

    up = [(i, i + 1) for i in range(devices - 1)]
    down = [(j, i) for i, j in up]
    halo_l = lax.ppermute(edge(slice(length - EDGE, length)), "slab", up)
    halo_r = lax.ppermute(edge(slice(0, EDGE)), "slab", down)
    ends = jnp.stack([me == 0, me == devices - 1]).astype(jnp.int32)

    x = exchange_rate
    keep = 1.0 - x
    powers = jnp.stack([jnp.ones_like(x), keep, keep * keep, keep * keep * keep])
    cx = capacity * x
    scal = jnp.concatenate([jnp.sum(cx)[None], jnp.sum(cx * x * powers, axis=1)])
    eye = jnp.eye(SPECIES, dtype=jnp.float32)
    sum_mat = ((cx * powers)[:, None, :, None] * eye[None, :, None, :]).reshape(
        TSTEPS * SPECIES, rows
    )
    s_hi, s_lo = split_mat(sum_mat)
    sum_mat = jnp.concatenate([s_hi, s_lo], axis=0)
    own = jnp.eye(CLASSES, dtype=jnp.float32) * (keep * keep * keep * keep)[:, None]
    own = (own[:, None, :, None] * eye[None, :, None, :]).reshape(rows, rows)
    feed = (x * powers[::-1]).T
    feed = (feed[:, None, :, None] * eye[None, :, None, :]).reshape(rows, TSTEPS * SPECIES)
    o_hi, o_lo = split_mat(own)
    f_hi, f_lo = split_mat(feed)
    out_mat = jnp.concatenate([o_hi, o_lo, f_hi, f_lo, f_hi], axis=1)

    chunk = next(c for c in (2048, 1536, 1024, 768, 512, 384, 256, 128) if length % c == 0)
    per = chunk // EDGE
    count = length // EDGE
    steps = length // chunk
    co = courant.reshape(1, length)

    def before(i):
        return jnp.maximum(i * per - 1, 0)

    def after(i):
        return jnp.minimum((i + 1) * per, count - 1)

    smem = pl.BlockSpec(memory_space=pltpu.SMEM)
    whole = lambda a: pl.BlockSpec(a.shape, lambda i: (0,) * a.ndim)
    return pl.pallas_call(
        transport_kernel,
        grid=(steps,),
        out_shape=(
            jax.ShapeDtypeStruct(mobile.shape, jnp.float32),
            jax.ShapeDtypeStruct(immobile.shape, jnp.bfloat16),
        ),
        in_specs=[
            smem,
            smem,
            whole(sum_mat),
            whole(out_mat),
            pl.BlockSpec((species, chunk), lambda i: (0, i)),
            pl.BlockSpec((species, EDGE), lambda i: (0, before(i))),
            pl.BlockSpec((species, EDGE), lambda i: (0, after(i))),
            pl.BlockSpec((CLASSES, species, chunk), lambda i: (0, 0, i)),
            pl.BlockSpec((CLASSES, species, EDGE), lambda i: (0, 0, before(i))),
            pl.BlockSpec((CLASSES, species, EDGE), lambda i: (0, 0, after(i))),
            pl.BlockSpec((1, chunk), lambda i: (0, i)),
            pl.BlockSpec((1, EDGE), lambda i: (0, before(i))),
            pl.BlockSpec((1, EDGE), lambda i: (0, after(i))),
            whole(halo_l),
            whole(halo_r),
        ],
        out_specs=(
            pl.BlockSpec((species, chunk), lambda i: (0, i)),
            pl.BlockSpec((CLASSES, species, chunk), lambda i: (0, 0, i)),
        ),
        compiler_params=pltpu.CompilerParams(vmem_limit_bytes=48 * 2**20),
        name="transport",
    )(
        ends, scal, sum_mat, out_mat, mobile, mobile, mobile, immobile, immobile, immobile,
        co, co, co, halo_l, halo_r,
    )


def substep(concs, qs, mat_full, mat_fast):
    us = list(concs)
    for turn in range(NEWTON):
        lin = []
        for u in us:
            hi = u.astype(jnp.bfloat16).astype(jnp.float32)
            lin.append(dot32(mat_full, jnp.concatenate([hi, u - hi, hi], axis=0).astype(jnp.bfloat16)))
        es, rs = [], []
        for u, c, q, hu in zip(us, concs, qs, lin):
            t = jnp.exp2(-jnp.abs(u))
            s = 1.0 + t
            soft = jnp.maximum(u, 0.0) + jnp.log2(s)
            if turn == 0:
                r = q * soft - hu
            else:
                r = (u - c) + (q * soft - hu)
            e = s * pl.reciprocal(s + q * jnp.where(u >= 0.0, 1.0, t), approx=True)
            es.append(e)
            rs.append(r)
        fast = [dot32(mat_fast, (e * r).astype(jnp.bfloat16)) for e, r in zip(es, rs)]
        us = [u - e * (r + f) for u, e, r, f in zip(us, es, rs, fast)]
    return us


def scan_heavy(kinds, order):
    def scan(i, n):
        @pl.when(kinds[i] == 1)
        def _():
            order[n] = i
        return n + jnp.where(kinds[i] == 1, 1, 0)

    return lax.fori_loop(0, kinds.shape[0], scan, jnp.int32(0))


def spot(index):
    return pl.ds(pl.multiple_of(index * BLOCK, BLOCK), BLOCK)


def share_of(heavy, peer):
    return (heavy + PEERS - peer) // (PEERS + 1)


def pack_kernel(kinds, m_ref, mask_ref, *rest):
    outs, order = rest[:PEERS + 1], rest[PEERS + 1]
    heavy = scan_heavy(kinds, order)
    for peer, out in enumerate(outs):
        n = share_of(heavy, peer)
        depth = out.shape[1] // BLOCK - 2
        out[...] = jnp.zeros_like(out)
        out[:, (depth + 1) * BLOCK:] = jnp.full((SPECIES, BLOCK), n, jnp.int32).astype(jnp.float32)

        @pl.loop(0, n)
        def _(j):
            b = order[j * (PEERS + 1) + peer]
            out[:, spot(j)] = m_ref[:, spot(b)]
            row = lax.broadcasted_iota(jnp.int32, (SPECIES, BLOCK), 0) == j
            masks = jnp.broadcast_to(mask_ref[:, spot(b)].astype(jnp.float32), (SPECIES, BLOCK))
            kept = out[:, depth * BLOCK:(depth + 1) * BLOCK]
            out[:, depth * BLOCK:(depth + 1) * BLOCK] = jnp.where(row, masks, kept)


def react_list(count, pick, src, mask, dst, full, fast, rates):
    def run(base, size):
        widths = ways_of(size)
        spots = [spot(pick(jnp.minimum(base + j, count - 1))) for j in range(size)]
        sides, at = [], 0
        for width in widths:
            sides.append(spots[at:at + width])
            at += width

        def side(ref, places):
            return jnp.concatenate([ref[:, p] for p in places], axis=1)

        cs = [side(src, p) * LOG2E for p in sides]
        qs = [rates * side(mask, p).astype(jnp.float32) for p in sides]
        done = lax.fori_loop(
            0, SUBSTEPS, lambda i, us: tuple(substep(us, qs, full[...], fast[...])), tuple(cs)
        )
        for p, u in zip(sides, done):
            for j, place in enumerate(p):
                dst[:, place] = u[:, j * BLOCK:(j + 1) * BLOCK] * LN2

    fulls = count // GROUP

    @pl.loop(0, fulls)
    def _(g):
        run(g * GROUP, GROUP)

    rest = count - fulls * GROUP
    for least, size in ((0, 8), (8, 16), (16, 24), (24, 32)):
        @pl.when((rest > least) & (rest <= size))
        def _(size=size):
            run(fulls * GROUP, size)


def light_kernel(full_l, fast_l, rates, m_ref, mask_ref, out_ref):
    count = m_ref.shape[1] // BLOCK
    p_light = rates[...] * reaction_step
    chunk = next(c for c in (32, 24, 16, 12, 8, 6, 4, 3, 2, 1) if count % c == 0)
    parts = ways_of(chunk)

    @pl.loop(0, count // chunk)
    def _(g):
        starts, at = [], 0
        for width in parts:
            starts.append((pl.multiple_of((g * chunk + at) * BLOCK, BLOCK), width * BLOCK))
            at += width
        cs = [m_ref[:, pl.ds(s, w)] * LOG2E for s, w in starts]
        qs = [p_light * mask_ref[:, pl.ds(s, w)].astype(jnp.float32) for s, w in starts]
        us = substep(cs, qs, full_l[...], fast_l[...])
        for (s, w), u in zip(starts, us):
            out_ref[:, pl.ds(s, w)] = u * LN2


def heavy_kernel(full_h, fast_h, rates, *rest):
    ins, outs = rest[:PEERS + 1], rest[PEERS + 1:2 * PEERS + 2]
    conc, mask = rest[2 * PEERS + 2:]
    p_heavy = rates[...] * (heavy_span / SUBSTEPS)
    depth = outs[0].shape[1] // BLOCK
    counts = [
        jnp.max(r[0:1, (depth + 1) * BLOCK:(depth + 2) * BLOCK]).astype(jnp.int32) for r in ins
    ]
    bases, total = [], jnp.int32(0)
    for n in counts:
        bases.append(total)
        total = total + n
    for ref, n, base in zip(ins, counts, bases):
        @pl.loop(0, n)
        def _(j, ref=ref, base=base):
            conc[:, spot(base + j)] = ref[:, spot(j)]
            row = lax.broadcasted_iota(jnp.int32, (SPECIES, BLOCK), 0) == j
            masks = jnp.where(row, ref[:, depth * BLOCK:(depth + 1) * BLOCK], 0.0)
            mask[:, spot(base + j)] = jnp.sum(masks, axis=0, keepdims=True)
    react_list(total, lambda j: j, conc, mask, conc, full_h, fast_h, p_heavy)
    for ref, n, base in zip(outs, counts, bases):
        ref[...] = jnp.zeros_like(ref)

        @pl.loop(0, n)
        def _(j, ref=ref, base=base):
            ref[:, spot(j)] = conc[:, spot(base + j)]


def merge_kernel(kinds, own_ref, *rest):
    backs, out_ref, order = rest[:PEERS + 1], rest[PEERS + 1], rest[PEERS + 2]
    heavy = scan_heavy(kinds, order)
    out_ref[...] = own_ref[...]
    for peer, back in enumerate(backs):
        @pl.loop(0, share_of(heavy, peer))
        def _(j, peer=peer, back=back):
            out_ref[:, spot(order[j * (PEERS + 1) + peer])] = back[:, spot(j)]


def ways_of(size):
    step = 8
    return [min(step, size - at) for at in range(0, size, step)]


def chem_mats(reaction):
    base = reaction - jnp.eye(SPECIES, dtype=jnp.float32)
    mats = []
    for h in (reaction_step, heavy_span / SUBSTEPS):
        hi, lo = split_mat(base * h)
        mats += [jnp.concatenate([hi, hi, lo], axis=1), hi]
    return mats


def chemistry(moving, block_class, precip_mask, reaction, precip_rate):
    species, length = moving.shape
    count = block_class.shape[0]
    devices = lax.axis_size("slab")
    depth = -(-count // (PEERS + 1))
    full_l, fast_l, full_h, fast_h = chem_mats(reaction)
    rates = precip_rate[:, None]
    mask = precip_mask.reshape(1, length)
    vmem = pl.BlockSpec(memory_space=pltpu.VMEM)
    smem = pl.BlockSpec(memory_space=pltpu.SMEM)
    order = pltpu.SMEM((count,), jnp.int32)
    params = pltpu.CompilerParams(vmem_limit_bytes=40 * 2**20)
    packed = jax.ShapeDtypeStruct((species, (depth + 2) * BLOCK), jnp.float32)
    slots = jax.ShapeDtypeStruct((species, depth * BLOCK), jnp.float32)
    whole = jax.ShapeDtypeStruct(moving.shape, jnp.float32)
    swaps = [[(i, i ^ bit) for i in range(devices)] for bit in (1, 2, 4)[:PEERS]]

    sent = pl.pallas_call(
        pack_kernel,
        out_shape=(packed,) * (PEERS + 1),
        in_specs=[smem, vmem, vmem],
        out_specs=(vmem,) * (PEERS + 1),
        scratch_shapes=[order],
        compiler_params=params,
        name="pack",
    )(block_class, moving, mask)
    guests = [lax.ppermute(x, "slab", swap) for x, swap in zip(sent[1:], swaps)]
    light = pl.pallas_call(
        light_kernel,
        out_shape=whole,
        in_specs=[vmem] * 5,
        out_specs=vmem,
        compiler_params=params,
        cost_estimate=pl.CostEstimate(
            flops=10**9, bytes_accessed=8 * species * length, transcendentals=10**6
        ),
        name="light",
    )(full_l, fast_l, rates, moving, mask)
    guests, light = lax.optimization_barrier((guests, light))
    reacted = pl.pallas_call(
        heavy_kernel,
        out_shape=(slots,) * (PEERS + 1),
        in_specs=[vmem] * (4 + PEERS),
        out_specs=(vmem,) * (PEERS + 1),
        scratch_shapes=[
            pltpu.VMEM((species, (PEERS + 1) * depth * BLOCK), jnp.float32),
            pltpu.VMEM((1, (PEERS + 1) * depth * BLOCK), jnp.float32),
        ],
        compiler_params=params,
        name="heavy",
    )(full_h, fast_h, rates, sent[0], *guests)
    backs = [lax.ppermute(x, "slab", swap) for x, swap in zip(reacted[1:], swaps)]
    return pl.pallas_call(
        merge_kernel,
        out_shape=whole,
        in_specs=[smem] + [vmem] * (2 + PEERS),
        out_specs=vmem,
        scratch_shapes=[order],
        compiler_params=params,
        name="merge",
    )(block_class, light, reacted[0], *backs)


def per_device(
    mobile, immobile, courant, exchange_rate, capacity, reaction, precip_rate, block_class,
    precip_mask,
):
    moving, immobile_out = transport(mobile, immobile, courant, exchange_rate, capacity)
    mobile_out = chemistry(moving, block_class, precip_mask, reaction, precip_rate)
    return (mobile_out, immobile_out)


def solution(mesh):
    in_specs = (
        P(None, ("groups", "slab")),
        P(None, None, ("groups", "slab")),
        P(("groups", "slab")),
        P(),
        P(),
        P(),
        P(),
        P(("groups", "slab")),
        P(("groups", "slab")),
    )
    out_specs = (P(None, ("groups", "slab")), P(None, None, ("groups", "slab")))
    return jax.shard_map(
        per_device, mesh=mesh, in_specs=in_specs, out_specs=out_specs, check_vma=False
    )
```

```python
from functools import partial

import jax
import jax.numpy as jnp
from jax import lax
from jax.experimental import pallas as pl
from jax.experimental.pallas import tpu as pltpu
from jax.sharding import PartitionSpec as P

BLOCK = 128
TSTEPS = 4
NEWTON = 3
SUBSTEPS = 20

dispersion = 0.05
reaction_step = 0.25
heavy_span = 4.0

EDGE = 128
LOG2E = 1.4426950408889634
LN2 = 0.6931471805599453
CLASSES = 8
SPECIES = 24
GROUP = 48
TAIL = 8
PEERS = 3


def split_hi_lo(x):
    hi = x.astype(jnp.bfloat16)
    lo = (x - hi.astype(jnp.float32)).astype(jnp.bfloat16)
    return hi, lo


def split_mat(x):
    hi = lax.reduce_precision(x, 8, 7)
    return hi.astype(jnp.bfloat16), (x - hi).astype(jnp.bfloat16)


def dot32(a, b):
    return jnp.dot(a, b, preferred_element_type=jnp.float32)


def transport_kernel(
    ends, scal, sum_mat, out_mat, m_c, m_l, m_r, n_c, n_l, n_r, co_c, co_l, co_r,
    halo_l, halo_r, m_out, n_out,
):
    step, steps = pl.program_id(0), pl.num_programs(0)
    chunk = m_c.shape[1]
    first, last = step == 0, step == steps - 1
    rows = CLASSES * SPECIES

    def flat(ref):
        return ref[...].astype(jnp.float32).reshape(rows, ref.shape[2])

    nl = jnp.where(first, halo_l[:rows, :], flat(n_l)).astype(jnp.bfloat16)
    nr = jnp.where(last, halo_r[:rows, :], flat(n_r)).astype(jnp.bfloat16)
    nc = flat(n_c).astype(jnp.bfloat16)
    ml = jnp.where(first, halo_l[rows:rows + SPECIES, :], m_l[...])
    mr = jnp.where(last, halo_r[rows:rows + SPECIES, :], m_r[...])
    cl = jnp.where(first, halo_l[rows + SPECIES:rows + SPECIES + 1, :], co_l[...])
    cr = jnp.where(last, halo_r[rows + SPECIES:rows + SPECIES + 1, :], co_r[...])
    wide = jnp.concatenate([nl, nc, nr], axis=1)
    m = jnp.concatenate([ml, m_c[...], mr], axis=1)
    co = jnp.concatenate([cl, co_c[...], cr], axis=1)
    width = chunk + 2 * EDGE
    lane = lax.broadcasted_iota(jnp.int32, (1, width), 1)
    out_left = (lane < EDGE) & first & (ends[0] == 1)
    out_right = (lane >= EDGE + chunk) & last & (ends[1] == 1)
    valid = jnp.where(out_left | out_right, 0.0, 1.0)
    total = scal[0]
    center_w = (1.0 - co - 2.0 * dispersion - total) * valid
    left_w = (co + dispersion) * valid
    right_w = dispersion * valid
    both = dot32(sum_mat[...], wide)
    sums = both[:TSTEPS * SPECIES] + both[TSTEPS * SPECIES:]
    past = []
    for t in range(TSTEPS):
        past.append(m)
        left = pltpu.roll(m, 1, axis=1)
        right = pltpu.roll(m, width - 1, axis=1)
        extra = sums[t * SPECIES:(t + 1) * SPECIES]
        for j in range(t):
            extra = extra + scal[1 + t - 1 - j] * past[j]
        m = center_w * m + left_w * left + right_w * right + extra * valid
    m_out[...] = m[:, EDGE:EDGE + chunk]
    inner = jnp.concatenate([p[:, EDGE:EDGE + chunk] for p in past], axis=0)
    hi, lo = split_hi_lo(inner)
    stack = jnp.concatenate([nc, nc, hi, hi, lo], axis=0)
    n_new = dot32(out_mat[...], stack)
    n_out[...] = n_new.reshape(CLASSES, SPECIES, chunk).astype(jnp.bfloat16)


def transport(mobile, immobile, courant, exchange_rate, capacity):
    species, length = mobile.shape
    devices = lax.axis_size("slab")
    me = lax.axis_index("slab")
    rows = CLASSES * SPECIES

    def edge(sl):
        return jnp.concatenate(
            [
                immobile[:, :, sl].astype(jnp.float32).reshape(rows, EDGE),
                mobile[:, sl],
                jnp.broadcast_to(courant[None, sl], (8, EDGE)),
            ],
            axis=0,
        )

    up = [(i, i + 1) for i in range(devices - 1)]
    down = [(j, i) for i, j in up]
    halo_l = lax.ppermute(edge(slice(length - EDGE, length)), "slab", up)
    halo_r = lax.ppermute(edge(slice(0, EDGE)), "slab", down)
    ends = jnp.stack([me == 0, me == devices - 1]).astype(jnp.int32)

    x = exchange_rate
    keep = 1.0 - x
    powers = jnp.stack([jnp.ones_like(x), keep, keep * keep, keep * keep * keep])
    cx = capacity * x
    scal = jnp.concatenate([jnp.sum(cx)[None], jnp.sum(cx * x * powers, axis=1)])
    eye = jnp.eye(SPECIES, dtype=jnp.float32)
    sum_mat = ((cx * powers)[:, None, :, None] * eye[None, :, None, :]).reshape(
        TSTEPS * SPECIES, rows
    )
    s_hi, s_lo = split_mat(sum_mat)
    sum_mat = jnp.concatenate([s_hi, s_lo], axis=0)
    own = jnp.eye(CLASSES, dtype=jnp.float32) * (keep * keep * keep * keep)[:, None]
    own = (own[:, None, :, None] * eye[None, :, None, :]).reshape(rows, rows)
    feed = (x * powers[::-1]).T
    feed = (feed[:, None, :, None] * eye[None, :, None, :]).reshape(rows, TSTEPS * SPECIES)
    o_hi, o_lo = split_mat(own)
    f_hi, f_lo = split_mat(feed)
    out_mat = jnp.concatenate([o_hi, o_lo, f_hi, f_lo, f_hi], axis=1)

    chunk = next(c for c in (2048, 1536, 1024, 768, 512, 384, 256, 128) if length % c == 0)
    per = chunk // EDGE
    count = length // EDGE
    steps = length // chunk
    co = courant.reshape(1, length)

    def before(i):
        return jnp.maximum(i * per - 1, 0)

    def after(i):
        return jnp.minimum((i + 1) * per, count - 1)

    smem = pl.BlockSpec(memory_space=pltpu.SMEM)
    whole = lambda a: pl.BlockSpec(a.shape, lambda i: (0,) * a.ndim)
    return pl.pallas_call(
        transport_kernel,
        grid=(steps,),
        out_shape=(
            jax.ShapeDtypeStruct(mobile.shape, jnp.float32),
            jax.ShapeDtypeStruct(immobile.shape, jnp.bfloat16),
        ),
        in_specs=[
            smem,
            smem,
            whole(sum_mat),
            whole(out_mat),
            pl.BlockSpec((species, chunk), lambda i: (0, i)),
            pl.BlockSpec((species, EDGE), lambda i: (0, before(i))),
            pl.BlockSpec((species, EDGE), lambda i: (0, after(i))),
            pl.BlockSpec((CLASSES, species, chunk), lambda i: (0, 0, i)),
            pl.BlockSpec((CLASSES, species, EDGE), lambda i: (0, 0, before(i))),
            pl.BlockSpec((CLASSES, species, EDGE), lambda i: (0, 0, after(i))),
            pl.BlockSpec((1, chunk), lambda i: (0, i)),
            pl.BlockSpec((1, EDGE), lambda i: (0, before(i))),
            pl.BlockSpec((1, EDGE), lambda i: (0, after(i))),
            whole(halo_l),
            whole(halo_r),
        ],
        out_specs=(
            pl.BlockSpec((species, chunk), lambda i: (0, i)),
            pl.BlockSpec((CLASSES, species, chunk), lambda i: (0, 0, i)),
        ),
        compiler_params=pltpu.CompilerParams(vmem_limit_bytes=48 * 2**20),
        name="transport",
    )(
        ends, scal, sum_mat, out_mat, mobile, mobile, mobile, immobile, immobile, immobile,
        co, co, co, halo_l, halo_r,
    )


def substep(concs, qs, mat_full, mat_fast):
    us = list(concs)
    for turn in range(NEWTON):
        lin = []
        for u in us:
            hi = u.astype(jnp.bfloat16).astype(jnp.float32)
            lin.append(dot32(mat_full, jnp.concatenate([hi, u - hi, hi], axis=0).astype(jnp.bfloat16)))
        es, rs = [], []
        for u, c, q, hu in zip(us, concs, qs, lin):
            t = jnp.exp2(-jnp.abs(u))
            s = 1.0 + t
            soft = jnp.maximum(u, 0.0) + jnp.log2(s)
            if turn == 0:
                r = q * soft - hu
            else:
                r = (u - c) + (q * soft - hu)
            e = s * pl.reciprocal(s + q * jnp.where(u >= 0.0, 1.0, t), approx=True)
            es.append(e)
            rs.append(r)
        fast = [dot32(mat_fast, (e * r).astype(jnp.bfloat16)) for e, r in zip(es, rs)]
        us = [u - e * (r + f) for u, e, r, f in zip(us, es, rs, fast)]
    return us


def scan_heavy(kinds, order):
    def scan(i, n):
        @pl.when(kinds[i] == 1)
        def _():
            order[n] = i
        return n + jnp.where(kinds[i] == 1, 1, 0)

    return lax.fori_loop(0, kinds.shape[0], scan, jnp.int32(0))


def spot(index):
    return pl.ds(pl.multiple_of(index * BLOCK, BLOCK), BLOCK)


def share_of(heavy, peer):
    return (heavy + PEERS - peer) // (PEERS + 1)


def pack_kernel(kinds, m_ref, mask_ref, *rest):
    outs, order = rest[:PEERS + 1], rest[PEERS + 1]
    heavy = scan_heavy(kinds, order)
    for peer, out in enumerate(outs):
        n = share_of(heavy, peer)
        depth = out.shape[1] // BLOCK - 2
        out[...] = jnp.zeros_like(out)
        out[:, (depth + 1) * BLOCK:] = jnp.full((SPECIES, BLOCK), n, jnp.int32).astype(jnp.float32)

        @pl.loop(0, n)
        def _(j):
            b = order[j * (PEERS + 1) + peer]
            out[:, spot(j)] = m_ref[:, spot(b)]
            row = lax.broadcasted_iota(jnp.int32, (SPECIES, BLOCK), 0) == j
            masks = jnp.broadcast_to(mask_ref[:, spot(b)].astype(jnp.float32), (SPECIES, BLOCK))
            kept = out[:, depth * BLOCK:(depth + 1) * BLOCK]
            out[:, depth * BLOCK:(depth + 1) * BLOCK] = jnp.where(row, masks, kept)


def react_list(count, pick, src, mask, dst, full, fast, rates):
    def run(base, size):
        widths = ways_of(size)
        spots = [spot(pick(jnp.minimum(base + j, count - 1))) for j in range(size)]
        sides, at = [], 0
        for width in widths:
            sides.append(spots[at:at + width])
            at += width

        def side(ref, places):
            return jnp.concatenate([ref[:, p] for p in places], axis=1)

        cs = [side(src, p) * LOG2E for p in sides]
        qs = [rates * side(mask, p).astype(jnp.float32) for p in sides]
        done = lax.fori_loop(
            0, SUBSTEPS, lambda i, us: tuple(substep(us, qs, full[...], fast[...])), tuple(cs)
        )
        for p, u in zip(sides, done):
            for j, place in enumerate(p):
                dst[:, place] = u[:, j * BLOCK:(j + 1) * BLOCK] * LN2

    fulls = jnp.maximum(count - 1, 0) // GROUP

    @pl.loop(0, fulls)
    def _(g):
        run(g * GROUP, GROUP)

    rest = count - fulls * GROUP
    for size in range(TAIL, GROUP + 1, TAIL):
        @pl.when((rest > size - TAIL) & (rest <= size))
        def _(size=size):
            run(fulls * GROUP, size)


def light_kernel(full_l, fast_l, rates, m_ref, mask_ref, out_ref):
    count = m_ref.shape[1] // BLOCK
    p_light = rates[...] * reaction_step
    chunk = next(c for c in (32, 24, 16, 12, 8, 6, 4, 3, 2, 1) if count % c == 0)
    parts = ways_of(chunk)

    @pl.loop(0, count // chunk)
    def _(g):
        starts, at = [], 0
        for width in parts:
            starts.append((pl.multiple_of((g * chunk + at) * BLOCK, BLOCK), width * BLOCK))
            at += width
        cs = [m_ref[:, pl.ds(s, w)] * LOG2E for s, w in starts]
        qs = [p_light * mask_ref[:, pl.ds(s, w)].astype(jnp.float32) for s, w in starts]
        us = substep(cs, qs, full_l[...], fast_l[...])
        for (s, w), u in zip(starts, us):
            out_ref[:, pl.ds(s, w)] = u * LN2


def heavy_kernel(full_h, fast_h, rates, *rest):
    ins, outs = rest[:PEERS + 1], rest[PEERS + 1:2 * PEERS + 2]
    conc, mask = rest[2 * PEERS + 2:]
    p_heavy = rates[...] * (heavy_span / SUBSTEPS)
    depth = outs[0].shape[1] // BLOCK
    counts = [
        jnp.max(r[0:1, (depth + 1) * BLOCK:(depth + 2) * BLOCK]).astype(jnp.int32) for r in ins
    ]
    bases, total = [], jnp.int32(0)
    for n in counts:
        bases.append(total)
        total = total + n
    for ref, n, base in zip(ins, counts, bases):
        @pl.loop(0, n)
        def _(j, ref=ref, base=base):
            conc[:, spot(base + j)] = ref[:, spot(j)]
            row = lax.broadcasted_iota(jnp.int32, (SPECIES, BLOCK), 0) == j
            masks = jnp.where(row, ref[:, depth * BLOCK:(depth + 1) * BLOCK], 0.0)
            mask[:, spot(base + j)] = jnp.sum(masks, axis=0, keepdims=True)
    react_list(total, lambda j: j, conc, mask, conc, full_h, fast_h, p_heavy)
    for ref, n, base in zip(outs, counts, bases):
        ref[...] = jnp.zeros_like(ref)

        @pl.loop(0, n)
        def _(j, ref=ref, base=base):
            ref[:, spot(j)] = conc[:, spot(base + j)]


def merge_kernel(kinds, own_ref, *rest):
    backs, out_ref, order = rest[:PEERS + 1], rest[PEERS + 1], rest[PEERS + 2]
    heavy = scan_heavy(kinds, order)
    out_ref[...] = own_ref[...]
    for peer, back in enumerate(backs):
        @pl.loop(0, share_of(heavy, peer))
        def _(j, peer=peer, back=back):
            out_ref[:, spot(order[j * (PEERS + 1) + peer])] = back[:, spot(j)]


def ways_of(size):
    step = 8
    return [min(step, size - at) for at in range(0, size, step)]


def chem_mats(reaction):
    base = reaction - jnp.eye(SPECIES, dtype=jnp.float32)
    mats = []
    for h in (reaction_step, heavy_span / SUBSTEPS):
        hi, lo = split_mat(base * h)
        mats += [jnp.concatenate([hi, hi, lo], axis=1), hi]
    return mats


def chemistry(moving, block_class, precip_mask, reaction, precip_rate):
    species, length = moving.shape
    count = block_class.shape[0]
    devices = lax.axis_size("slab")
    depth = -(-count // (PEERS + 1))
    full_l, fast_l, full_h, fast_h = chem_mats(reaction)
    rates = precip_rate[:, None]
    mask = precip_mask.reshape(1, length)
    vmem = pl.BlockSpec(memory_space=pltpu.VMEM)
    smem = pl.BlockSpec(memory_space=pltpu.SMEM)
    order = pltpu.SMEM((count,), jnp.int32)
    params = pltpu.CompilerParams(vmem_limit_bytes=40 * 2**20)
    packed = jax.ShapeDtypeStruct((species, (depth + 2) * BLOCK), jnp.float32)
    slots = jax.ShapeDtypeStruct((species, depth * BLOCK), jnp.float32)
    whole = jax.ShapeDtypeStruct(moving.shape, jnp.float32)
    swaps = [[(i, i ^ bit) for i in range(devices)] for bit in (1, 2, 4)[:PEERS]]

    sent = pl.pallas_call(
        pack_kernel,
        out_shape=(packed,) * (PEERS + 1),
        in_specs=[smem, vmem, vmem],
        out_specs=(vmem,) * (PEERS + 1),
        scratch_shapes=[order],
        compiler_params=params,
        name="pack",
    )(block_class, moving, mask)
    guests = [lax.ppermute(x, "slab", swap) for x, swap in zip(sent[1:], swaps)]
    light = pl.pallas_call(
        light_kernel,
        out_shape=whole,
        in_specs=[vmem] * 5,
        out_specs=vmem,
        compiler_params=params,
        cost_estimate=pl.CostEstimate(
            flops=10**9, bytes_accessed=8 * species * length, transcendentals=10**6
        ),
        name="light",
    )(full_l, fast_l, rates, moving, mask)
    guests, light = lax.optimization_barrier((guests, light))
    reacted = pl.pallas_call(
        heavy_kernel,
        out_shape=(slots,) * (PEERS + 1),
        in_specs=[vmem] * (4 + PEERS),
        out_specs=(vmem,) * (PEERS + 1),
        scratch_shapes=[
            pltpu.VMEM((species, (PEERS + 1) * depth * BLOCK), jnp.float32),
            pltpu.VMEM((1, (PEERS + 1) * depth * BLOCK), jnp.float32),
        ],
        compiler_params=params,
        name="heavy",
    )(full_h, fast_h, rates, sent[0], *guests)
    backs = [lax.ppermute(x, "slab", swap) for x, swap in zip(reacted[1:], swaps)]
    return pl.pallas_call(
        merge_kernel,
        out_shape=whole,
        in_specs=[smem] + [vmem] * (2 + PEERS),
        out_specs=vmem,
        scratch_shapes=[order],
        compiler_params=params,
        name="merge",
    )(block_class, light, reacted[0], *backs)


def per_device(
    mobile, immobile, courant, exchange_rate, capacity, reaction, precip_rate, block_class,
    precip_mask,
):
    moving, immobile_out = transport(mobile, immobile, courant, exchange_rate, capacity)
    mobile_out = chemistry(moving, block_class, precip_mask, reaction, precip_rate)
    return (mobile_out, immobile_out)


def solution(mesh):
    in_specs = (
        P(None, ("groups", "slab")),
        P(None, None, ("groups", "slab")),
        P(("groups", "slab")),
        P(),
        P(),
        P(),
        P(),
        P(("groups", "slab")),
        P(("groups", "slab")),
    )
    out_specs = (P(None, ("groups", "slab")), P(None, None, ("groups", "slab")))
    return jax.shard_map(
        per_device, mesh=mesh, in_specs=in_specs, out_specs=out_specs, check_vma=False
    )
```
